32 devices in a mesh: gx: 4 (over y, core), gy: 8 (over z, x).
Axes of the slice: x: 2, y: 2, z: 4, core: 2. Of those that a mesh axis runs over, the one named last changes fastest.
Arguments:
- pressure_init: float32 [64, 256, 128], P('gx', 'gy'), may hold values from -6 to 6
- source: float32 [64, 256, 128], P('gx', 'gy'), may hold values from -6 to 6
- permeability: float32 [64, 256, 128], P('gx', 'gy'), may hold values from 0.1 to 10
Outputs:
- pressure: float32 [64, 256, 128], P('gx', 'gy')
- correction_mid: float32 [32, 128, 128], P('gx', 'gy')
- correction_coarse: float32 [16, 64, 128], P('gx', 'gy')
The draws below stay inside these ranges and needn't reach their ends.
All inputs are finite; a program needn't handle non-finite values.
Results may differ from the reference program's by a relative error of at most 0.0003.
Values sent between devices are 32-bit elements; how exact they have to be, the bound alone decides.
A program may use at most 64 MiB of HBM per device.

```python
import math
import jax
import jax.numpy as jnp

NZ = 128
SWEEPS = 2
COARSE = 4
NX = 64
NY = 256


def steps_of(key, extent, shards, low, largest):
    def one(dim, blocks):
        draws = jax.random.uniform(jax.random.fold_in(jax.random.fold_in(key, 6), dim), (blocks,), jnp.float32, low / len(shards), largest / len(shards))
        return jnp.repeat(jnp.exp(draws), extent[dim] // blocks).reshape((-1,) + (1,) * (len(extent) - dim - 1))

    level = one(*shards[0])
    for cut in shards[1:]:
        level = level * one(*cut)
    return level


def scatter_about(own_key, extent, width, bound, pieces=(), dtype=jnp.bfloat16):
    result = width * jax.random.normal(own_key, extent, jnp.float32)
    if pieces:
        result = result * steps_of(own_key, extent, pieces, -0.22, 0.18)
    return jnp.clip(result, -bound, bound).astype(dtype)


def setup_inputs(seed: int = 0) -> dict:
    streams_of = jax.random.split(jax.random.key(seed), 4)
    return {
        "pressure_init": scatter_about(streams_of[0], (NX, NY, NZ), 1.0, 6.0, ((0, 4), (1, 8)), jnp.float32),
        "source": scatter_about(streams_of[1], (NX, NY, NZ), 1.0, 6.0, ((0, 4), (1, 8)), jnp.float32),
        "permeability": jnp.clip(jnp.exp(math.log(10.0) - 4.6051702 * jax.random.uniform(streams_of[2], (NX, NY, NZ), jnp.float32) ** steps_of(streams_of[2], (NX, NY, NZ), ((0, 4), (1, 8)), -0.2, 0.2)), 0.1, 10.0),
    }


STORE = 0.1
OMEGA = 0.8


def harmonic(first, second):
    total = first + second
    return 2.0 * first * second / jnp.where(total > 0, total, 1.0)


def widths(axis, low):
    pads = [(0, 0), (0, 0), (0, 0)]
    pads[axis] = (1, 0) if low else (0, 1)
    return pads


def face_sum(coupling, axis):
    return jnp.pad(coupling, widths(axis, True)) + jnp.pad(coupling, widths(axis, False))


def net_flow(flow, axis):
    return jnp.pad(flow, widths(axis, False)) - jnp.pad(flow, widths(axis, True))


def coefficients(perm, scale):
    couple_x = scale * harmonic(perm[1:], perm[:-1])
    couple_y = scale * harmonic(perm[:, 1:], perm[:, :-1])
    couple_z = harmonic(perm[:, :, 1:], perm[:, :, :-1])
    diagonal = STORE + face_sum(couple_x, 0) + face_sum(couple_y, 1) + face_sum(couple_z, 2)
    return couple_x, couple_y, couple_z, diagonal


def apply_operator(value, parts):
    couple_x, couple_y, couple_z, diagonal = parts
    flow_x = couple_x * (value[:-1] - value[1:])
    flow_y = couple_y * (value[:, :-1] - value[:, 1:])
    flow_z = couple_z * (value[:, :, :-1] - value[:, :, 1:])
    return STORE * value + net_flow(flow_x, 0) + net_flow(flow_y, 1) + net_flow(flow_z, 2)


def restrict(field):
    sx, sy, sz = field.shape
    return 0.25 * jnp.sum(field.reshape(sx // 2, 2, sy // 2, 2, sz), axis=(1, 3))


def smooth_zero(rhs, parts, sweeps):
    value = OMEGA * rhs / parts[3]
    for step in range(sweeps - 1):
        value = value + OMEGA * (rhs - apply_operator(value, parts)) / parts[3]
    return value


def reference(pressure_init, source, permeability):
    parts0 = coefficients(permeability, 1.0)
    pressure = pressure_init
    for step in range(SWEEPS):
        pressure = pressure + OMEGA * (source - apply_operator(pressure, parts0)) / parts0[3]
    resid0 = source - apply_operator(pressure, parts0)
    rhs_mid = restrict(resid0)
    perm_mid = restrict(permeability)
    parts1 = coefficients(perm_mid, 0.25)
    correction_mid = smooth_zero(rhs_mid, parts1, SWEEPS)
    resid1 = rhs_mid - apply_operator(correction_mid, parts1)
    rhs_coarse = restrict(resid1)
    parts2 = coefficients(restrict(perm_mid), 0.0625)
    correction_coarse = smooth_zero(rhs_coarse, parts2, COARSE)
    return pressure, correction_mid, correction_coarse
```

```python
import functools

import jax
import jax.numpy as jnp
from jax import lax
from jax.experimental import pallas as pl
from jax.experimental.pallas import tpu as pltpu
from jax.sharding import PartitionSpec as P

STORE = 0.1
OMEGA = 0.8
MESH = pl.DeviceIdType.MESH
DIRS = ((-1, 0), (1, 0), (0, -1), (0, 1), (-1, -1), (-1, 1), (1, -1), (1, 1))
CHUNK = 2


def hm(a, b):
    return 2.0 * a * b / jnp.maximum(a + b, 1e-30)


def over_planes(lo, hi, fn, chunk=CHUNK):
    whole = (hi - lo) // chunk

    def step(t, carry):
        fn(lo + t * chunk, chunk)
        return carry

    if whole:
        lax.fori_loop(0, whole, step, 0)
    if (hi - lo) % chunk:
        fn(lo + whole * chunk, (hi - lo) % chunk)


def rolls(rows):
    def y_next(v):
        return pltpu.roll(v, rows - 1, 1)

    def y_prev(v):
        return pltpu.roll(v, 1, 1)

    def z_next(v):
        return pltpu.roll(v, 127, 2)

    def z_prev(v):
        return pltpu.roll(v, 1, 2)

    return y_next, y_prev, z_next, z_prev


def make_coefficients(k, cx, cy, cz, w, d, scale):
    planes, rows, _ = k.shape
    y_next, y_prev, z_next, z_prev = rolls(rows)
    cx[0] = scale * hm(k[0], k[1])

    def fn(i, n):
        here = k[pl.ds(i, n)]
        x = scale * hm(here, k[pl.ds(i + 1, n)])
        cx[pl.ds(i, n)] = x
        y = scale * hm(here, y_next(here))
        cy[pl.ds(i, n)] = y
        z = hm(here, z_next(here))
        lane = lax.broadcasted_iota(jnp.int32, z.shape, 2)
        z = jnp.where(lane < 127, z, 0.0)
        cz[pl.ds(i, n)] = z
        diag = STORE + x + cx[pl.ds(i - 1, n)] + y + y_prev(y) + z + z_prev(z)
        d[pl.ds(i, n)] = diag
        w[pl.ds(i, n)] = OMEGA / diag

    over_planes(1, planes - 1, fn)


def neighbour_sum(v, cx, cy, cz, i, n):
    y_next, y_prev, z_next, z_prev = rolls(v.shape[1])
    here = v[pl.ds(i, n)]
    y = cy[pl.ds(i, n)]
    z = cz[pl.ds(i, n)]
    total = cx[pl.ds(i, n)] * v[pl.ds(i + 1, n)] + cx[pl.ds(i - 1, n)] * v[pl.ds(i - 1, n)]
    total = total + (y * y_next(here) + y_prev(y * here))
    total = total + (z * z_next(here) + z_prev(z * here))
    return here, total


def sweep(src, dst, b, cx, cy, cz, w, lo, hi):
    def fn(i, n):
        here, total = neighbour_sum(src, cx, cy, cz, i, n)
        dst[pl.ds(i, n)] = (1.0 - OMEGA) * here + w[pl.ds(i, n)] * (b[pl.ds(i, n)] + total)

    over_planes(lo, hi, fn)


def restrict(src, off, tmp, dst, dst_off, cx_, cy_):
    for i in range(cx_):
        tmp[i] = 0.25 * (src[off + 2 * i, 0 : 2 * cy_] + src[off + 2 * i + 1, 0 : 2 * cy_])
        dst[dst_off + i, 0:cy_] = tmp[i, pl.ds(0, cy_, stride=2)] + tmp[i, pl.ds(1, cy_, stride=2)]


def edge_rows(extent, width, step):
    return range(extent - width, extent) if step > 0 else range(width)


def halo_rows(extent, rows, width, step):
    return range(rows - width, rows) if step > 0 else range(extent, extent + width)


def halo_planes(extent, off, width, step):
    return range(off - width, off) if step > 0 else range(off + extent, off + extent + width)


def flat(ref):
    planes, rows, lanes = ref.shape
    return ref.reshape(planes * rows, lanes)


def zero_halo(ref, extent_x, extent_y, off):
    planes, rows, lanes = ref.shape
    ref[0:off] = jnp.zeros((off, rows, lanes), jnp.float32)
    ref[off + extent_x : planes] = jnp.zeros((planes - off - extent_x, rows, lanes), jnp.float32)
    ref[off : off + extent_x, extent_y:rows] = jnp.zeros((extent_x, rows - extent_y, lanes), jnp.float32)


def kernel(
    p_in, s_in, k_in, p_out, c1_out, c2_out,
    k0, p0, s0, p1, p2, cx0, cy0, cz0, w0, d0,
    k1, b1, u1, v1, cx1, cy1, cz1, w1, d1,
    k2, b2, u2, v2, cx2, cy2, cz2, w2, d2,
    r0, r1, t0, t1,
    ya, yar, ca, car, yb, ybr, cb, cbr, yc, ycr, cc, ccr, yd, ydr, cd, cdr,
    lsem, ssem, rsem,
):
    X, Y = p_in.shape[0], p_in.shape[1]
    nx, ny = lax.axis_size("gx"), lax.axis_size("gy")
    gx, gy = lax.axis_index("gx"), lax.axis_index("gy")
    H0, H1, H2 = 3, 3, 4
    X1, Y1, X2, Y2 = X // 2, Y // 2, X // 4, Y // 4

    def exists(d):
        dx, dy = d
        ok = None
        for coord, step, size in ((gx, dx, nx), (gy, dy, ny)):
            if step:
                one = (coord + step >= 0) & (coord + step < size)
                ok = one if ok is None else ok & one
        return ok

    here = {d: exists(d) for d in DIRS}

    def opposite(d):
        return (-d[0], -d[1])

    local = [
        pltpu.make_async_copy(src, dst.at[H0 : H0 + X, 0:Y], lsem.at[i])
        for i, (src, dst) in enumerate(((k_in, k0), (p_in, p0), (s_in, s0)))
    ]
    for copy in local:
        copy.start()
    for ref in (k0, p0, s0):
        zero_halo(ref, X, Y, H0)
    for ref in (k1, b1):
        zero_halo(ref, X1, Y1, H1)
    for ref in (k2, b2):
        zero_halo(ref, X2, Y2, H2)

    barrier = pltpu.get_barrier_semaphore()
    for d in DIRS:

        @pl.when(here[d])
        def _():
            pl.semaphore_signal(
                barrier, inc=1, device_id={"gx": gx + d[0], "gy": gy + d[1]}, device_id_type=MESH
            )

    one = lambda d: here[d].astype(jnp.int32)
    count = one(DIRS[0])
    for d in DIRS[1:]:
        count = count + one(d)
    pl.semaphore_wait(barrier, count)

    counter = [0]
    every = []

    def message(d, src, dst):
        slot = counter[0]
        counter[0] += 1
        copy = pltpu.make_async_remote_copy(
            src_ref=src, dst_ref=dst, send_sem=ssem.at[slot], recv_sem=rsem.at[slot],
            device_id={"gx": gx + d[0], "gy": gy + d[1]}, device_id_type=MESH,
        )

        @pl.when(here[d])
        def _():
            copy.start()

        every.append((d, copy))
        return d, copy

    def receive(messages):
        for d, copy in messages:

            @pl.when(here[opposite(d)])
            def _():
                copy.wait_recv()

    def part(ref, planes, rows):
        return ref.at[planes.start : planes.stop, 0:rows]

    def tile_planes(extent, width, step):
        edge = edge_rows(extent, width, step)
        return edge

    sent_a = []
    for d in ((-1, 0), (1, 0)):
        for src, dst, width in ((k_in, k0, 3), (p_in, p0, 3), (s_in, s0, 2)):
            planes = edge_rows(X, width, d[0])
            sent_a.append(
                message(d, src.at[planes.start : planes.stop], part(dst, halo_planes(X, H0, width, d[0]), Y))
            )
    for copy in local:
        copy.wait()
    R0, R1, R2 = k0.shape[1], k1.shape[1], k2.shape[1]
    arrays_a = ((k0, 3), (p0, 3), (s0, 2))
    for j, dy in enumerate((-1, 1)):
        slot = 0
        for ref, width in arrays_a:
            for y in edge_rows(Y, width, dy):
                ya[j, slot] = flat(ref)[pl.ds(H0 * R0 + y, X, stride=R0), :]
                slot += 1
        sent_a.append(message((0, dy), ya.at[j], yar.at[j]))

    def pack_corner(stage, j, slot, ref, off, ex, ey, width, d):
        ys = edge_rows(ey, width, d[1])
        for x in edge_rows(ex, width, d[0]):
            stage[j, slot : slot + width] = ref[off + x, ys.start : ys.stop]
            slot += width
        return slot

    def unpack_corner(stage, j, slot, ref, off, ex, ey, width, d):
        ys = halo_rows(ey, ref.shape[1], width, d[1])
        for x in halo_planes(ex, off, width, d[0]):
            ref[x, ys.start : ys.stop] = stage[j, slot : slot + width]
            slot += width
        return slot

    corners_a = ((k0, 2), (p0, 2), (s0, 1))
    for j, d in enumerate(DIRS[4:]):
        slot = 0
        for ref, width in corners_a:
            slot = pack_corner(ca, j, slot, ref, H0, X, Y, width, d)
        sent_a.append(message(d, ca.at[j], car.at[j]))

    restrict(k0, H0, t0, k1, H1, X1, Y1)
    restrict(k1, H1, t1, k2, H2, X2, Y2)
    sent_b = []
    for d in ((-1, 0), (1, 0)):
        for ref, off, ex, ey, width in ((k1, H1, X1, Y1, 3), (k2, H2, X2, Y2, 4)):
            planes = edge_rows(ex, width, d[0])
            src = ref.at[off + planes.start : off + planes.stop, 0:ey]
            sent_b.append(message(d, src, part(ref, halo_planes(ex, off, width, d[0]), ey)))
    for j, dy in enumerate((-1, 1)):
        slot = 0
        for y in edge_rows(Y1, 3, dy):
            yb[j, slot : slot + X1] = flat(k1)[pl.ds(H1 * R1 + y, X1, stride=R1), :]
            slot += X1
        for y in edge_rows(Y2, 4, dy):
            yb[j, slot : slot + X2] = flat(k2)[pl.ds(H2 * R2 + y, X2, stride=R2), :]
            slot += X2
        sent_b.append(message((0, dy), yb.at[j], ybr.at[j]))
    for j, d in enumerate(DIRS[4:]):
        slot = pack_corner(cb, j, 0, k1, H1, X1, Y1, 2, d)
        pack_corner(cb, j, slot, k2, H2, X2, Y2, 3, d)
        sent_b.append(message(d, cb.at[j], cbr.at[j]))

    receive(sent_a)
    for j, dy in enumerate((-1, 1)):

        @pl.when(here[(0, -dy)])
        def _():
            slot = 0
            for ref, width in arrays_a:
                for y in halo_rows(Y, R0, width, dy):
                    flat(ref)[pl.ds(H0 * R0 + y, X, stride=R0), :] = yar[j, slot]
                    slot += 1

    for j, d in enumerate(DIRS[4:]):

        @pl.when(here[opposite(d)])
        def _():
            slot = 0
            for ref, width in corners_a:
                slot = unpack_corner(car, j, slot, ref, H0, X, Y, width, d)

    make_coefficients(k0, cx0, cy0, cz0, w0, d0, 1.0)
    sweep(p0, p1, s0, cx0, cy0, cz0, w0, 1, X + 5)
    sweep(p1, p2, s0, cx0, cy0, cz0, w0, 2, X + 4)

    def residual0(i, n):
        value, total = neighbour_sum(p2, cx0, cy0, cz0, i, n)
        p_out[pl.ds(i - H0, n)] = value[:, 0:Y]
        r = s0[pl.ds(i, n)] + total - d0[pl.ds(i, n)] * value
        r0[pl.ds(i - H0, n)] = r[:, 0:Y]

    over_planes(H0, H0 + X, residual0)
    restrict(r0, 0, t0, b1, H1, X1, Y1)

    sent_c = []
    for d in ((-1, 0), (1, 0)):
        planes = edge_rows(X1, 2, d[0])
        src = b1.at[H1 + planes.start : H1 + planes.stop, 0:Y1]
        sent_c.append(message(d, src, part(b1, halo_planes(X1, H1, 2, d[0]), Y1)))
    for j, dy in enumerate((-1, 1)):
        for slot, y in enumerate(edge_rows(Y1, 2, dy)):
            yc[j, slot] = flat(b1)[pl.ds(H1 * R1 + y, X1, stride=R1), :]
        sent_c.append(message((0, dy), yc.at[j], ycr.at[j]))
    for j, d in enumerate(DIRS[4:]):
        pack_corner(cc, j, 0, b1, H1, X1, Y1, 1, d)
        sent_c.append(message(d, cc.at[j], ccr.at[j]))

    receive(sent_b)
    for j, dy in enumerate((-1, 1)):

        @pl.when(here[(0, -dy)])
        def _():
            slot = 0
            for y in halo_rows(Y1, R1, 3, dy):
                flat(k1)[pl.ds(H1 * R1 + y, X1, stride=R1), :] = ybr[j, slot : slot + X1]
                slot += X1
            for y in halo_rows(Y2, R2, 4, dy):
                flat(k2)[pl.ds(H2 * R2 + y, X2, stride=R2), :] = ybr[j, slot : slot + X2]
                slot += X2

    for j, d in enumerate(DIRS[4:]):

        @pl.when(here[opposite(d)])
        def _():
            slot = unpack_corner(cbr, j, 0, k1, H1, X1, Y1, 2, d)
            unpack_corner(cbr, j, slot, k2, H2, X2, Y2, 3, d)

    make_coefficients(k1, cx1, cy1, cz1, w1, d1, 0.25)
    make_coefficients(k2, cx2, cy2, cz2, w2, d2, 0.0625)

    receive(sent_c)
    for j, dy in enumerate((-1, 1)):

        @pl.when(here[(0, -dy)])
        def _():
            for slot, y in enumerate(halo_rows(Y1, R1, 2, dy)):
                flat(b1)[pl.ds(H1 * R1 + y, X1, stride=R1), :] = ycr[j, slot]

    for j, d in enumerate(DIRS[4:]):

        @pl.when(here[opposite(d)])
        def _():
            unpack_corner(ccr, j, 0, b1, H1, X1, Y1, 1, d)

    u1[1 : X1 + 5] = w1[1 : X1 + 5] * b1[1 : X1 + 5]
    sweep(u1, v1, b1, cx1, cy1, cz1, w1, 2, X1 + 4)

    def residual1(i, n):
        value, total = neighbour_sum(v1, cx1, cy1, cz1, i, n)
        c1_out[pl.ds(i - H1, n)] = value[:, 0:Y1]
        r = b1[pl.ds(i, n)] + total - d1[pl.ds(i, n)] * value
        r1[pl.ds(i - H1, n)] = r[:, 0:Y1]

    over_planes(H1, H1 + X1, residual1)
    restrict(r1, 0, t1, b2, H2, X2, Y2)

    sent_d = []
    for d in ((-1, 0), (1, 0)):
        planes = edge_rows(X2, 3, d[0])
        src = b2.at[H2 + planes.start : H2 + planes.stop, 0:Y2]
        sent_d.append(message(d, src, part(b2, halo_planes(X2, H2, 3, d[0]), Y2)))
    for j, dy in enumerate((-1, 1)):
        for slot, y in enumerate(edge_rows(Y2, 3, dy)):
            yd[j, slot * X2 : slot * X2 + X2] = flat(b2)[pl.ds(H2 * R2 + y, X2, stride=R2), :]
        sent_d.append(message((0, dy), yd.at[j], ydr.at[j]))
    for j, d in enumerate(DIRS[4:]):
        pack_corner(cd, j, 0, b2, H2, X2, Y2, 2, d)
        sent_d.append(message(d, cd.at[j], cdr.at[j]))
    receive(sent_d)
    for j, dy in enumerate((-1, 1)):

        @pl.when(here[(0, -dy)])
        def _():
            for slot, y in enumerate(halo_rows(Y2, R2, 3, dy)):
                flat(b2)[pl.ds(H2 * R2 + y, X2, stride=R2), :] = ydr[j, slot * X2 : slot * X2 + X2]

    for j, d in enumerate(DIRS[4:]):

        @pl.when(here[opposite(d)])
        def _():
            unpack_corner(cdr, j, 0, b2, H2, X2, Y2, 2, d)

    u2[1 : X2 + 7] = w2[1 : X2 + 7] * b2[1 : X2 + 7]
    sweep(u2, v2, b2, cx2, cy2, cz2, w2, 2, X2 + 6)
    sweep(v2, u2, b2, cx2, cy2, cz2, w2, 3, X2 + 5)
    value, total = neighbour_sum(u2, cx2, cy2, cz2, H2, X2)
    value = (1.0 - OMEGA) * value + w2[H2 : H2 + X2] * (b2[H2 : H2 + X2] + total)
    c2_out[...] = value[:, 0:Y2]

    for d, copy in every:

        @pl.when(here[d])
        def _():
            copy.wait_send()


MESSAGES = 12 + 10 + 8 + 8


def body(pressure_init, source, permeability):
    X, Y, Z = permeability.shape
    f32 = jnp.float32

    def vmem(*shape):
        return pltpu.VMEM(shape, f32)

    def level(x, y, off):
        return (x + 2 * off, y + 8, Z)

    l0, l1, l2 = level(X, Y, 3), level(X // 2, Y // 2, 3), level(X // 4, Y // 4, 4)
    scratch = (
        [vmem(*l0)] * 10
        + [vmem(*l1)] * 9
        + [vmem(*l2)] * 9
        + [vmem(X, Y, Z), vmem(X // 2, Y // 2, Z), vmem(X // 2, Y, Z), vmem(X // 4, Y // 2, Z)]
        + [vmem(2, 8, X, Z)] * 2
        + [vmem(4, 16, Z)] * 2
        + [vmem(2, 3 * (X // 2) + 4 * (X // 4), Z)] * 2
        + [vmem(4, 16, Z)] * 2
        + [vmem(2, 2, X // 2, Z)] * 2
        + [vmem(4, 8, Z)] * 2
        + [vmem(2, 16, Z)] * 2
        + [vmem(4, 8, Z)] * 2
        + [
            pltpu.SemaphoreType.DMA((3,)),
            pltpu.SemaphoreType.DMA((MESSAGES,)),
            pltpu.SemaphoreType.DMA((MESSAGES,)),
        ]
    )
    return pl.pallas_call(
        kernel,
        out_shape=(
            jax.ShapeDtypeStruct((X, Y, Z), f32),
            jax.ShapeDtypeStruct((X // 2, Y // 2, Z), f32),
            jax.ShapeDtypeStruct((X // 4, Y // 4, Z), f32),
        ),
        in_specs=[pl.BlockSpec(memory_space=pl.ANY)] * 3,
        out_specs=[pl.BlockSpec(memory_space=pltpu.VMEM)] * 3,
        scratch_shapes=scratch,
        compiler_params=pltpu.CompilerParams(
            collective_id=0, has_side_effects=True, vmem_limit_bytes=32 * 1024 * 1024
        ),
    )(pressure_init, source, permeability)


def solution(mesh):
    spec = P("gx", "gy", None)
    return jax.shard_map(
        body, mesh=mesh, in_specs=(spec,) * 3, out_specs=(spec,) * 3, check_vma=False
    )
```

```python
import functools

import jax
import jax.numpy as jnp
from jax import lax
from jax.experimental import pallas as pl
from jax.experimental.pallas import tpu as pltpu
from jax.sharding import PartitionSpec as P

STORE = 0.1
OMEGA = 0.8
MESH = pl.DeviceIdType.MESH
DIRS = ((-1, 0), (1, 0), (0, -1), (0, 1), (-1, -1), (-1, 1), (1, -1), (1, 1))
CHUNK = 8


def hm(a, b):
    return 2.0 * a * b / jnp.maximum(a + b, 1e-30)


def over_planes(lo, hi, fn, chunk=CHUNK):
    for i in range(lo, hi, chunk):
        fn(i, min(chunk, hi - i))


def rolls(rows):
    def y_next(v):
        return pltpu.roll(v, rows - 1, 1)

    def y_prev(v):
        return pltpu.roll(v, 1, 1)

    def z_next(v):
        return pltpu.roll(v, 127, 2)

    def z_prev(v):
        return pltpu.roll(v, 1, 2)

    return y_next, y_prev, z_next, z_prev


def make_coefficients(k, cx, cy, cz, w, d, scale):
    planes, rows, _ = k.shape
    y_next, y_prev, z_next, z_prev = rolls(rows)
    cx[0] = scale * hm(k[0], k[1])

    def fn(i, n):
        here = k[pl.ds(i, n)]
        x = scale * hm(here, k[pl.ds(i + 1, n)])
        cx[pl.ds(i, n)] = x
        y = scale * hm(here, y_next(here))
        cy[pl.ds(i, n)] = y
        z = hm(here, z_next(here))
        lane = lax.broadcasted_iota(jnp.int32, z.shape, 2)
        z = jnp.where(lane < 127, z, 0.0)
        cz[pl.ds(i, n)] = z
        diag = STORE + x + cx[pl.ds(i - 1, n)] + y + y_prev(y) + z + z_prev(z)
        d[pl.ds(i, n)] = diag
        w[pl.ds(i, n)] = OMEGA / diag

    over_planes(1, planes - 1, fn)


def neighbour_sum(v, cx, cy, cz, i, n):
    y_next, y_prev, z_next, z_prev = rolls(v.shape[1])
    here = v[pl.ds(i, n)]
    y = cy[pl.ds(i, n)]
    z = cz[pl.ds(i, n)]
    total = cx[pl.ds(i, n)] * v[pl.ds(i + 1, n)] + cx[pl.ds(i - 1, n)] * v[pl.ds(i - 1, n)]
    total = total + (y * y_next(here) + y_prev(y * here))
    total = total + (z * z_next(here) + z_prev(z * here))
    return here, total


def sweep(src, dst, b, cx, cy, cz, w, lo, hi):
    def fn(i, n):
        here, total = neighbour_sum(src, cx, cy, cz, i, n)
        dst[pl.ds(i, n)] = (1.0 - OMEGA) * here + w[pl.ds(i, n)] * (b[pl.ds(i, n)] + total)

    over_planes(lo, hi, fn)


def restrict(src, off, tmp, dst, dst_off, cx_, cy_):
    for i in range(cx_):
        tmp[i] = 0.25 * (src[off + 2 * i, 0 : 2 * cy_] + src[off + 2 * i + 1, 0 : 2 * cy_])
        dst[dst_off + i, 0:cy_] = tmp[i, pl.ds(0, cy_, stride=2)] + tmp[i, pl.ds(1, cy_, stride=2)]


def edge_rows(extent, width, step):
    return range(extent - width, extent) if step > 0 else range(width)


def halo_rows(extent, rows, width, step):
    return range(rows - width, rows) if step > 0 else range(extent, extent + width)


def halo_planes(extent, off, width, step):
    return range(off - width, off) if step > 0 else range(off + extent, off + extent + width)


def flat(ref):
    planes, rows, lanes = ref.shape
    return ref.reshape(planes * rows, lanes)


def zero_halo(ref, extent_x, extent_y, off, width, low, high):
    planes, rows, lanes = ref.shape

    def zero(start, stop, first, last):
        if stop > start:
            ref[start:stop, first:last] = jnp.zeros((stop - start, last - first, lanes), jnp.float32)

    zero(0, planes, extent_y, rows)
    zero(0, off - width, 0, extent_y)
    zero(off + extent_x + width, planes, 0, extent_y)

    @pl.when(jnp.logical_not(low))
    def _():
        zero(off - width, off, 0, extent_y)

    @pl.when(jnp.logical_not(high))
    def _():
        zero(off + extent_x, off + extent_x + width, 0, extent_y)


def kernel(
    p_in, s_in, k_in, p_out, c1_out, b2, cx2, cy2, cz2, w2,
    k0, p0, s0, p1, p2, cx0, cy0, cz0, w0, d0,
    k1, b1, u1, v1, cx1, cy1, cz1, w1, d1,
    k2, d2,
    r0, r1, t0, t1,
    ya, yar, ca, car, yc, ycr, cc, ccr, yd, ydr, cd, cdr,
    lsem, ssem, rsem,
):
    X, Y = p_in.shape[0], p_in.shape[1]
    nx, ny = lax.axis_size("gx"), lax.axis_size("gy")
    gx, gy = lax.axis_index("gx"), lax.axis_index("gy")
    H0, H1, H2 = 3, 3, 4
    X1, Y1, X2, Y2 = X // 2, Y // 2, X // 4, Y // 4

    def exists(d):
        dx, dy = d
        ok = None
        for coord, step, size in ((gx, dx, nx), (gy, dy, ny)):
            if step:
                one = (coord + step >= 0) & (coord + step < size)
                ok = one if ok is None else ok & one
        return ok

    here = {d: exists(d) for d in DIRS}

    def opposite(d):
        return (-d[0], -d[1])

    barrier = pltpu.get_barrier_semaphore()
    for d in DIRS:

        @pl.when(here[d])
        def _():
            pl.semaphore_signal(
                barrier, inc=1, device_id={"gx": gx + d[0], "gy": gy + d[1]}, device_id_type=MESH
            )

    local = [
        pltpu.make_async_copy(src, dst.at[H0 : H0 + X, 0:Y], lsem.at[i])
        for i, (src, dst) in enumerate(((k_in, k0), (p_in, p0), (s_in, s0)))
    ]
    for copy in local:
        copy.start()
    low, high = here[(-1, 0)], here[(1, 0)]
    zero_halo(k0, X, Y, H0, 3, low, high)
    zero_halo(p0, X, Y, H0, 3, low, high)
    zero_halo(s0, X, Y, H0, 2, low, high)
    zero_halo(k1, X1, Y1, H1, 3, low, high)
    zero_halo(b1, X1, Y1, H1, 2, low, high)
    zero_halo(k2, X2, Y2, H2, 4, low, high)
    zero_halo(b2, X2, Y2, H2, 3, low, high)

    counter = [0]
    every = []

    def message(d, src, dst):
        slot = counter[0]
        counter[0] += 1
        copy = pltpu.make_async_remote_copy(
            src_ref=src, dst_ref=dst, send_sem=ssem.at[slot], recv_sem=rsem.at[slot],
            device_id={"gx": gx + d[0], "gy": gy + d[1]}, device_id_type=MESH,
        )

        @pl.when(here[d])
        def _():
            copy.start()

        every.append((d, copy))
        return d, copy

    def receive(messages):
        for d, copy in messages:

            @pl.when(here[opposite(d)])
            def _():
                copy.wait_recv()

    def part(ref, planes, rows):
        return ref.at[planes.start : planes.stop, 0:rows]

    R0, R1, R2 = k0.shape[1], k1.shape[1], k2.shape[1]

    def pack_side(stage, j, slot, ref, off, ex, ey, width, dy):
        for y in edge_rows(ey, width, dy):
            stage[j, slot : slot + ex] = flat(ref)[pl.ds(off * ref.shape[1] + y, ex, stride=ref.shape[1]), :]
            slot += ex
        return slot

    def unpack_side(stage, j, slot, ref, off, ex, ey, width, dy):
        for y in halo_rows(ey, ref.shape[1], width, dy):
            flat(ref)[pl.ds(off * ref.shape[1] + y, ex, stride=ref.shape[1]), :] = stage[j, slot : slot + ex]
            slot += ex
        return slot

    def pack_corner(stage, j, slot, ref, off, ex, ey, width, d):
        ys = edge_rows(ey, width, d[1])
        for x in edge_rows(ex, width, d[0]):
            stage[j, slot : slot + width] = ref[off + x, ys.start : ys.stop]
            slot += width
        return slot

    def unpack_corner(stage, j, slot, ref, off, ex, ey, width, d):
        ys = halo_rows(ey, ref.shape[1], width, d[1])
        for x in halo_planes(ex, off, width, d[0]):
            ref[x, ys.start : ys.stop] = stage[j, slot : slot + width]
            slot += width
        return slot

    def pack(arrays, side, corner):
        for j, dy in enumerate((-1, 1)):
            slot = 0
            for ref, off, ex, ey, width, _ in arrays:
                slot = pack_side(side, j, slot, ref, off, ex, ey, width, dy)
        for j, d in enumerate(DIRS[4:]):
            slot = 0
            for ref, off, ex, ey, _, width in arrays:
                slot = pack_corner(corner, j, slot, ref, off, ex, ey, width, d)

    def unpack(arrays, side, corner):
        for j, dy in enumerate((-1, 1)):

            @pl.when(here[(0, -dy)])
            def _():
                slot = 0
                for ref, off, ex, ey, width, _ in arrays:
                    slot = unpack_side(side, j, slot, ref, off, ex, ey, width, dy)

        for j, d in enumerate(DIRS[4:]):

            @pl.when(here[opposite(d)])
            def _():
                slot = 0
                for ref, off, ex, ey, _, width in arrays:
                    slot = unpack_corner(corner, j, slot, ref, off, ex, ey, width, d)

    def send(arrays, side, side_in, corner, corner_in):
        sent = []
        for j, dy in enumerate((-1, 1)):
            sent.append(message((0, dy), side.at[j], side_in.at[j]))
        for j, d in enumerate(DIRS[4:]):
            sent.append(message(d, corner.at[j], corner_in.at[j]))
        for d in DIRS[:2]:
            for ref, off, ex, ey, width, _ in arrays:
                planes = edge_rows(ex, width, d[0])
                src = ref.at[off + planes.start : off + planes.stop, 0:ey]
                sent.append(message(d, src, part(ref, halo_planes(ex, off, width, d[0]), ey)))
        return sent

    arrays_a = (
        (k0, H0, X, Y, 3, 2), (p0, H0, X, Y, 3, 2), (s0, H0, X, Y, 2, 1),
        (k1, H1, X1, Y1, 3, 2), (k2, H2, X2, Y2, 4, 3),
    )
    arrays_c = ((b1, H1, X1, Y1, 2, 1),)
    arrays_d = ((b2, H2, X2, Y2, 3, 2),)
    for copy in local:
        copy.wait()
    restrict(k0, H0, t0, k1, H1, X1, Y1)
    restrict(k1, H1, t1, k2, H2, X2, Y2)
    pack(arrays_a, ya, ca)
    one = lambda d: here[d].astype(jnp.int32)
    count = one(DIRS[0])
    for d in DIRS[1:]:
        count = count + one(d)
    pl.semaphore_wait(barrier, count)

    sent_a = send(arrays_a, ya, yar, ca, car)

    receive(sent_a)
    unpack(arrays_a, yar, car)
    make_coefficients(k0, cx0, cy0, cz0, w0, d0, 1.0)
    sweep(p0, p1, s0, cx0, cy0, cz0, w0, 1, X + 5)
    sweep(p1, p2, s0, cx0, cy0, cz0, w0, 2, X + 4)

    def residual0(i, n):
        value, total = neighbour_sum(p2, cx0, cy0, cz0, i, n)
        p_out[pl.ds(i - H0, n)] = value[:, 0:Y]
        r = s0[pl.ds(i, n)] + total - d0[pl.ds(i, n)] * value
        r0[pl.ds(i - H0, n)] = r[:, 0:Y]

    over_planes(H0, H0 + X, residual0)
    restrict(r0, 0, t0, b1, H1, X1, Y1)

    pack(arrays_c, yc, cc)
    sent_c = send(arrays_c, yc, ycr, cc, ccr)
    make_coefficients(k1, cx1, cy1, cz1, w1, d1, 0.25)
    make_coefficients(k2, cx2, cy2, cz2, w2, d2, 0.0625)

    receive(sent_c)
    unpack(arrays_c, ycr, ccr)
    u1[1 : X1 + 5] = w1[1 : X1 + 5] * b1[1 : X1 + 5]
    sweep(u1, v1, b1, cx1, cy1, cz1, w1, 2, X1 + 4)

    def residual1(i, n):
        value, total = neighbour_sum(v1, cx1, cy1, cz1, i, n)
        c1_out[pl.ds(i - H1, n)] = value[:, 0:Y1]
        r = b1[pl.ds(i, n)] + total - d1[pl.ds(i, n)] * value
        r1[pl.ds(i - H1, n)] = r[:, 0:Y1]

    over_planes(H1, H1 + X1, residual1)
    restrict(r1, 0, t1, b2, H2, X2, Y2)

    pack(arrays_d, yd, cd)
    sent_d = send(arrays_d, yd, ydr, cd, cdr)
    receive(sent_d)
    unpack(arrays_d, ydr, cdr)

    for d, copy in every:

        @pl.when(here[d])
        def _():
            copy.wait_send()


def finish(p_in, c1_in, b2, cx2, cy2, cz2, w2, p_out, c1_out, c2_out, u2, v2, c2, sem):
    off = (b2.shape[0] - c2.shape[0]) // 2
    X2, Y2 = c2.shape[0], c2.shape[1]
    first = pltpu.make_async_copy(p_in, p_out, sem.at[0])
    second = pltpu.make_async_copy(c1_in, c1_out, sem.at[1])
    first.start()
    second.start()
    u2[0] = jnp.zeros(u2.shape[1:], jnp.float32)
    u2[X2 + 7] = jnp.zeros(u2.shape[1:], jnp.float32)
    u2[1 : X2 + 7] = w2[1 : X2 + 7] * b2[1 : X2 + 7]
    sweep(u2, v2, b2, cx2, cy2, cz2, w2, 2, X2 + 6)
    sweep(v2, u2, b2, cx2, cy2, cz2, w2, 3, X2 + 5)
    value, total = neighbour_sum(u2, cx2, cy2, cz2, off, X2)
    value = (1.0 - OMEGA) * value + w2[off : off + X2] * (b2[off : off + X2] + total)
    c2[...] = value[:, 0:Y2]
    third = pltpu.make_async_copy(c2, c2_out, sem.at[2])
    third.start()
    first.wait()
    second.wait()
    third.wait()


MESSAGES = 16 + 8 + 8


def body(pressure_init, source, permeability):
    X, Y, Z = permeability.shape
    f32 = jnp.float32

    def vmem(*shape):
        return pltpu.VMEM(shape, f32)

    def level(x, y, off):
        return (x + 2 * off, y + 8, Z)

    l0, l1, l2 = level(X, Y, 3), level(X // 2, Y // 2, 3), level(X // 4, Y // 4, 4)
    scratch = (
        [vmem(*l0)] * 10
        + [vmem(*l1)] * 9
        + [vmem(*l2)] * 2
        + [vmem(X, Y, Z), vmem(X // 2, Y // 2, Z), vmem(X // 2, Y, Z), vmem(X // 4, Y // 2, Z)]
        + [vmem(2, 8 * X + 3 * (X // 2) + 4 * (X // 4), Z)] * 2
        + [vmem(4, 24, Z)] * 2
        + [vmem(2, 2 * (X // 2), Z)] * 2
        + [vmem(4, 8, Z)] * 2
        + [vmem(2, 16, Z)] * 2
        + [vmem(4, 8, Z)] * 2
        + [
            pltpu.SemaphoreType.DMA((3,)),
            pltpu.SemaphoreType.DMA((MESSAGES,)),
            pltpu.SemaphoreType.DMA((MESSAGES,)),
        ]
    )
    def out(*shape):
        return jax.ShapeDtypeStruct(shape, f32)

    whole = pl.BlockSpec(memory_space=pltpu.VMEM)
    far = pl.BlockSpec(memory_space=pltpu.HBM)
    fine, mid, coarse = out(X, Y, Z), out(X // 2, Y // 2, Z), out(X // 4, Y // 4, Z)
    parts = pl.pallas_call(
        kernel,
        out_shape=(fine, mid) + (out(*l2),) * 5,
        in_specs=[far] * 3,
        out_specs=[whole] * 7,
        scratch_shapes=scratch,
        compiler_params=pltpu.CompilerParams(
            collective_id=0, has_side_effects=True, vmem_limit_bytes=53 * 1024 * 1024
        ),
    )(pressure_init, source, permeability)
    return pl.pallas_call(
        finish,
        out_shape=(fine, mid, coarse),
        in_specs=[whole] * 7,
        out_specs=[far] * 3,
        scratch_shapes=[vmem(*l2), vmem(*l2), vmem(X // 4, Y // 4, Z), pltpu.SemaphoreType.DMA((3,))],
        compiler_params=pltpu.CompilerParams(vmem_limit_bytes=16 * 1024 * 1024),
    )(*parts)


def solution(mesh):
    spec = P("gx", "gy", None)
    return jax.shard_map(
        body, mesh=mesh, in_specs=(spec,) * 3, out_specs=(spec,) * 3, check_vma=False
    )
```

```python
import functools

import jax
import jax.numpy as jnp
from jax import lax
from jax.experimental import pallas as pl
from jax.experimental.pallas import tpu as pltpu
from jax.sharding import PartitionSpec as P

STORE = 0.1
OMEGA = 0.8
MESH = pl.DeviceIdType.MESH
DIRS = ((-1, 0), (1, 0), (0, -1), (0, 1), (-1, -1), (-1, 1), (1, -1), (1, 1))
CHUNK = 8


def hm(a, b):
    return 2.0 * a * b / jnp.maximum(a + b, 1e-30)


def over_planes(lo, hi, fn, chunk=CHUNK):
    for i in range(lo, hi, chunk):
        fn(i, min(chunk, hi - i))


def rolls(rows):
    def y_next(v):
        return pltpu.roll(v, rows - 1, 1)

    def y_prev(v):
        return pltpu.roll(v, 1, 1)

    def z_next(v):
        return pltpu.roll(v, 127, 2)

    def z_prev(v):
        return pltpu.roll(v, 1, 2)

    return y_next, y_prev, z_next, z_prev


def make_coefficients(k, cx, cy, cz, w, d, scale):
    planes, rows, _ = k.shape
    y_next, y_prev, z_next, z_prev = rolls(rows)
    cx[0] = scale * hm(k[0], k[1])

    def fn(i, n):
        here = k[pl.ds(i, n)]
        x = scale * hm(here, k[pl.ds(i + 1, n)])
        cx[pl.ds(i, n)] = x
        y = scale * hm(here, y_next(here))
        cy[pl.ds(i, n)] = y
        z = hm(here, z_next(here))
        lane = lax.broadcasted_iota(jnp.int32, z.shape, 2)
        z = jnp.where(lane < 127, z, 0.0)
        cz[pl.ds(i, n)] = z
        diag = STORE + x + cx[pl.ds(i - 1, n)] + y + y_prev(y) + z + z_prev(z)
        d[pl.ds(i, n)] = diag
        w[pl.ds(i, n)] = OMEGA / diag

    over_planes(1, planes - 1, fn)


def neighbour_sum(v, cx, cy, cz, i, n):
    y_next, y_prev, z_next, z_prev = rolls(v.shape[1])
    here = v[pl.ds(i, n)]
    y = cy[pl.ds(i, n)]
    z = cz[pl.ds(i, n)]
    total = cx[pl.ds(i, n)] * v[pl.ds(i + 1, n)] + cx[pl.ds(i - 1, n)] * v[pl.ds(i - 1, n)]
    total = total + (y * y_next(here) + y_prev(y * here))
    total = total + (z * z_next(here) + z_prev(z * here))
    return here, total


def sweep(src, dst, b, cx, cy, cz, w, lo, hi):
    def fn(i, n):
        here, total = neighbour_sum(src, cx, cy, cz, i, n)
        dst[pl.ds(i, n)] = (1.0 - OMEGA) * here + w[pl.ds(i, n)] * (b[pl.ds(i, n)] + total)

    over_planes(lo, hi, fn)


def restrict(src, off, tmp, dst, dst_off, cx_, cy_):
    for i in range(cx_):
        tmp[i] = 0.25 * (src[off + 2 * i, 0 : 2 * cy_] + src[off + 2 * i + 1, 0 : 2 * cy_])
        dst[dst_off + i, 0:cy_] = tmp[i, pl.ds(0, cy_, stride=2)] + tmp[i, pl.ds(1, cy_, stride=2)]


def edge_rows(extent, width, step):
    return range(extent - width, extent) if step > 0 else range(width)


def halo_rows(extent, rows, width, step):
    return range(rows - width, rows) if step > 0 else range(extent, extent + width)


def halo_planes(extent, off, width, step):
    return range(off - width, off) if step > 0 else range(off + extent, off + extent + width)


def flat(ref):
    planes, rows, lanes = ref.shape
    return ref.reshape(planes * rows, lanes)


def zero_halo(ref, extent_x, extent_y, off, width, low, high):
    planes, rows, lanes = ref.shape

    def zero(start, stop, first, last):
        if stop > start:
            ref[start:stop, first:last] = jnp.zeros((stop - start, last - first, lanes), jnp.float32)

    zero(0, planes, extent_y, rows)
    zero(0, off - width, 0, extent_y)
    zero(off + extent_x + width, planes, 0, extent_y)

    @pl.when(jnp.logical_not(low))
    def _():
        zero(off - width, off, 0, extent_y)

    @pl.when(jnp.logical_not(high))
    def _():
        zero(off + extent_x, off + extent_x + width, 0, extent_y)


def kernel(
    p_in, s_in, k_in, p_out, c1_out, b2, cx2, cy2, cz2, w2,
    k0, p0, s0, p1, p2, cx0, cy0, cz0, w0, d0,
    k1, b1, u1, v1, cx1, cy1, cz1, w1, d1,
    k2, d2,
    r0, r1, t0, t1,
    yk, ykr, yv, yvr, ym, ymr, ca, car, yc, ycr, cc, ccr, yd, ydr, cd, cdr,
    lsem, ssem, rsem,
):
    X, Y = p_in.shape[0], p_in.shape[1]
    nx, ny = lax.axis_size("gx"), lax.axis_size("gy")
    gx, gy = lax.axis_index("gx"), lax.axis_index("gy")
    H0, H1, H2 = 3, 3, 4
    X1, Y1, X2, Y2 = X // 2, Y // 2, X // 4, Y // 4

    def exists(d):
        dx, dy = d
        ok = None
        for coord, step, size in ((gx, dx, nx), (gy, dy, ny)):
            if step:
                one = (coord + step >= 0) & (coord + step < size)
                ok = one if ok is None else ok & one
        return ok

    here = {d: exists(d) for d in DIRS}

    def opposite(d):
        return (-d[0], -d[1])

    barrier = pltpu.get_barrier_semaphore()
    for d in DIRS:

        @pl.when(here[d])
        def _():
            pl.semaphore_signal(
                barrier, inc=1, device_id={"gx": gx + d[0], "gy": gy + d[1]}, device_id_type=MESH
            )

    local = [
        pltpu.make_async_copy(src, dst.at[H0 : H0 + X, 0:Y], lsem.at[i])
        for i, (src, dst) in enumerate(((k_in, k0), (p_in, p0), (s_in, s0)))
    ]
    for copy in local:
        copy.start()
    low, high = here[(-1, 0)], here[(1, 0)]
    zero_halo(k0, X, Y, H0, 3, low, high)
    zero_halo(p0, X, Y, H0, 3, low, high)
    zero_halo(s0, X, Y, H0, 2, low, high)
    zero_halo(k1, X1, Y1, H1, 3, low, high)
    zero_halo(b1, X1, Y1, H1, 2, low, high)
    zero_halo(k2, X2, Y2, H2, 4, low, high)
    zero_halo(b2, X2, Y2, H2, 3, low, high)

    counter = [0]

    def message(d, src, dst):
        slot = counter[0]
        counter[0] += 1
        copy = pltpu.make_async_remote_copy(
            src_ref=src, dst_ref=dst, send_sem=ssem.at[slot], recv_sem=rsem.at[slot],
            device_id={"gx": gx + d[0], "gy": gy + d[1]}, device_id_type=MESH,
        )

        @pl.when(here[d])
        def _():
            copy.start()

        return d, copy

    def receive(messages):
        for d, copy in messages:

            @pl.when(here[opposite(d)])
            def _():
                copy.wait_recv()

    def drain(messages):
        for d, copy in messages:

            @pl.when(here[d])
            def _():
                copy.wait_send()

    def part(ref, planes, rows):
        return ref.at[planes.start : planes.stop, 0:rows]

    R0, R1, R2 = k0.shape[1], k1.shape[1], k2.shape[1]

    def pack_side(stage, j, slot, ref, off, ex, ey, width, dy):
        for y in edge_rows(ey, width, dy):
            stage[j, slot : slot + ex] = flat(ref)[pl.ds(off * ref.shape[1] + y, ex, stride=ref.shape[1]), :]
            slot += ex
        return slot

    def unpack_side(stage, j, slot, ref, off, ex, ey, width, dy):
        for y in halo_rows(ey, ref.shape[1], width, dy):
            flat(ref)[pl.ds(off * ref.shape[1] + y, ex, stride=ref.shape[1]), :] = stage[j, slot : slot + ex]
            slot += ex
        return slot

    def pack_corner(stage, j, slot, ref, off, ex, ey, width, d):
        ys = edge_rows(ey, width, d[1])
        for x in edge_rows(ex, width, d[0]):
            stage[j, slot : slot + width] = ref[off + x, ys.start : ys.stop]
            slot += width
        return slot

    def unpack_corner(stage, j, slot, ref, off, ex, ey, width, d):
        ys = halo_rows(ey, ref.shape[1], width, d[1])
        for x in halo_planes(ex, off, width, d[0]):
            ref[x, ys.start : ys.stop] = stage[j, slot : slot + width]
            slot += width
        return slot

    def pack_sides(arrays, side):
        for j, dy in enumerate((-1, 1)):
            slot = 0
            for ref, off, ex, ey, width, _ in arrays:
                slot = pack_side(side, j, slot, ref, off, ex, ey, width, dy)

    def pack_corners(arrays, corner):
        for j, d in enumerate(DIRS[4:]):
            slot = 0
            for ref, off, ex, ey, _, width in arrays:
                slot = pack_corner(corner, j, slot, ref, off, ex, ey, width, d)

    def unpack_sides(arrays, side):
        for j, dy in enumerate((-1, 1)):

            @pl.when(here[(0, -dy)])
            def _():
                slot = 0
                for ref, off, ex, ey, width, _ in arrays:
                    slot = unpack_side(side, j, slot, ref, off, ex, ey, width, dy)

    def unpack_corners(arrays, corner):
        for j, d in enumerate(DIRS[4:]):

            @pl.when(here[opposite(d)])
            def _():
                slot = 0
                for ref, off, ex, ey, _, width in arrays:
                    slot = unpack_corner(corner, j, slot, ref, off, ex, ey, width, d)

    def send_sides(side, side_in):
        return [message((0, dy), side.at[j], side_in.at[j]) for j, dy in enumerate((-1, 1))]

    def send_corners(corner, corner_in):
        return [message(d, corner.at[j], corner_in.at[j]) for j, d in enumerate(DIRS[4:])]

    def send_planes(arrays):
        sent = []
        for ref, off, ex, ey, width, _ in arrays:
            for d in DIRS[:2]:
                planes = edge_rows(ex, width, d[0])
                src = ref.at[off + planes.start : off + planes.stop, 0:ey]
                sent.append(message(d, src, part(ref, halo_planes(ex, off, width, d[0]), ey)))
        return sent

    arrays_k = ((k0, H0, X, Y, 3, 2),)
    arrays_v = ((p0, H0, X, Y, 3, 2), (s0, H0, X, Y, 2, 1))
    arrays_m = ((k1, H1, X1, Y1, 3, 2), (k2, H2, X2, Y2, 4, 3))
    arrays_a = arrays_k + arrays_v + arrays_m
    arrays_c = ((b1, H1, X1, Y1, 2, 1),)
    arrays_d = ((b2, H2, X2, Y2, 3, 2),)
    for copy in local:
        copy.wait()
    restrict(k0, H0, t0, k1, H1, X1, Y1)
    restrict(k1, H1, t1, k2, H2, X2, Y2)
    pack_corners(arrays_a, ca)
    pack_sides(arrays_k, yk)
    pack_sides(arrays_v, yv)
    pack_sides(arrays_m, ym)
    one = lambda d: here[d].astype(jnp.int32)
    count = one(DIRS[0])
    for d in DIRS[1:]:
        count = count + one(d)
    pl.semaphore_wait(barrier, count)

    sent_k = send_corners(ca, car) + send_sides(yk, ykr) + send_planes(arrays_k)
    sent_v = send_sides(yv, yvr) + send_planes(arrays_v)
    sent_m = send_sides(ym, ymr) + send_planes(arrays_m)

    receive(sent_k)
    unpack_corners(arrays_a, car)
    unpack_sides(arrays_k, ykr)
    make_coefficients(k0, cx0, cy0, cz0, w0, d0, 1.0)
    receive(sent_v)
    unpack_sides(arrays_v, yvr)
    sweep(p0, p1, s0, cx0, cy0, cz0, w0, 1, X + 5)
    sweep(p1, p2, s0, cx0, cy0, cz0, w0, 2, X + 4)

    def residual0(i, n):
        value, total = neighbour_sum(p2, cx0, cy0, cz0, i, n)
        p_out[pl.ds(i - H0, n)] = value[:, 0:Y]
        r = s0[pl.ds(i, n)] + total - d0[pl.ds(i, n)] * value
        r0[pl.ds(i - H0, n)] = r[:, 0:Y]

    over_planes(H0, H0 + X, residual0)
    restrict(r0, 0, t0, b1, H1, X1, Y1)

    pack_corners(arrays_c, cc)
    pack_sides(arrays_c, yc)
    sent_c = send_corners(cc, ccr) + send_sides(yc, ycr) + send_planes(arrays_c)
    receive(sent_m)
    unpack_sides(arrays_m, ymr)
    make_coefficients(k1, cx1, cy1, cz1, w1, d1, 0.25)
    make_coefficients(k2, cx2, cy2, cz2, w2, d2, 0.0625)

    drain(sent_k + sent_v + sent_m)
    receive(sent_c)
    unpack_corners(arrays_c, ccr)
    unpack_sides(arrays_c, ycr)
    u1[1 : X1 + 5] = w1[1 : X1 + 5] * b1[1 : X1 + 5]
    sweep(u1, v1, b1, cx1, cy1, cz1, w1, 2, X1 + 4)

    def residual1(i, n):
        value, total = neighbour_sum(v1, cx1, cy1, cz1, i, n)
        c1_out[pl.ds(i - H1, n)] = value[:, 0:Y1]
        r = b1[pl.ds(i, n)] + total - d1[pl.ds(i, n)] * value
        r1[pl.ds(i - H1, n)] = r[:, 0:Y1]

    over_planes(H1, H1 + X1, residual1)
    restrict(r1, 0, t1, b2, H2, X2, Y2)

    pack_corners(arrays_d, cd)
    pack_sides(arrays_d, yd)
    sent_d = send_corners(cd, cdr) + send_sides(yd, ydr) + send_planes(arrays_d)
    drain(sent_c)
    receive(sent_d)
    unpack_corners(arrays_d, cdr)
    unpack_sides(arrays_d, ydr)

    drain(sent_d)


def finish(p_in, c1_in, b2, cx2, cy2, cz2, w2, p_out, c1_out, c2_out, u2, v2, c2, sem):
    off = (b2.shape[0] - c2.shape[0]) // 2
    X2, Y2 = c2.shape[0], c2.shape[1]
    first = pltpu.make_async_copy(p_in, p_out, sem.at[0])
    second = pltpu.make_async_copy(c1_in, c1_out, sem.at[1])
    first.start()
    second.start()
    u2[0] = jnp.zeros(u2.shape[1:], jnp.float32)
    u2[X2 + 7] = jnp.zeros(u2.shape[1:], jnp.float32)
    u2[1 : X2 + 7] = w2[1 : X2 + 7] * b2[1 : X2 + 7]
    sweep(u2, v2, b2, cx2, cy2, cz2, w2, 2, X2 + 6)
    sweep(v2, u2, b2, cx2, cy2, cz2, w2, 3, X2 + 5)
    value, total = neighbour_sum(u2, cx2, cy2, cz2, off, X2)
    value = (1.0 - OMEGA) * value + w2[off : off + X2] * (b2[off : off + X2] + total)
    c2[...] = value[:, 0:Y2]
    third = pltpu.make_async_copy(c2, c2_out, sem.at[2])
    third.start()
    first.wait()
    second.wait()
    third.wait()


MESSAGES = 20 + 8 + 8


def body(pressure_init, source, permeability):
    X, Y, Z = permeability.shape
    f32 = jnp.float32

    def vmem(*shape):
        return pltpu.VMEM(shape, f32)

    def level(x, y, off):
        return (x + 2 * off, y + 8, Z)

    l0, l1, l2 = level(X, Y, 3), level(X // 2, Y // 2, 3), level(X // 4, Y // 4, 4)
    scratch = (
        [vmem(*l0)] * 10
        + [vmem(*l1)] * 9
        + [vmem(*l2)] * 2
        + [vmem(X, Y, Z), vmem(X // 2, Y // 2, Z), vmem(X // 2, Y, Z), vmem(X // 4, Y // 2, Z)]
        + [vmem(2, 3 * X, Z)] * 2
        + [vmem(2, 5 * X, Z)] * 2
        + [vmem(2, 3 * (X // 2) + 4 * (X // 4), Z)] * 2
        + [vmem(4, 24, Z)] * 2
        + [vmem(2, 2 * (X // 2), Z)] * 2
        + [vmem(4, 8, Z)] * 2
        + [vmem(2, 16, Z)] * 2
        + [vmem(4, 8, Z)] * 2
        + [
            pltpu.SemaphoreType.DMA((3,)),
            pltpu.SemaphoreType.DMA((MESSAGES,)),
            pltpu.SemaphoreType.DMA((MESSAGES,)),
        ]
    )
    def out(*shape):
        return jax.ShapeDtypeStruct(shape, f32)

    whole = pl.BlockSpec(memory_space=pltpu.VMEM)
    far = pl.BlockSpec(memory_space=pltpu.HBM)
    fine, mid, coarse = out(X, Y, Z), out(X // 2, Y // 2, Z), out(X // 4, Y // 4, Z)
    parts = pl.pallas_call(
        kernel,
        out_shape=(fine, mid) + (out(*l2),) * 5,
        in_specs=[far] * 3,
        out_specs=[whole] * 7,
        scratch_shapes=scratch,
        compiler_params=pltpu.CompilerParams(
            collective_id=0, has_side_effects=True, vmem_limit_bytes=53 * 1024 * 1024
        ),
    )(pressure_init, source, permeability)
    return pl.pallas_call(
        finish,
        out_shape=(fine, mid, coarse),
        in_specs=[whole] * 7,
        out_specs=[far] * 3,
        scratch_shapes=[vmem(*l2), vmem(*l2), vmem(X // 4, Y // 4, Z), pltpu.SemaphoreType.DMA((3,))],
        compiler_params=pltpu.CompilerParams(vmem_limit_bytes=16 * 1024 * 1024),
    )(*parts)


def solution(mesh):
    spec = P("gx", "gy", None)
    return jax.shard_map(
        body, mesh=mesh, in_specs=(spec,) * 3, out_specs=(spec,) * 3, check_vma=False
    )
```

```python
import functools

import jax
import jax.numpy as jnp
from jax import lax
from jax.experimental import pallas as pl
from jax.experimental.pallas import tpu as pltpu
from jax.sharding import PartitionSpec as P

STORE = 0.1
OMEGA = 0.8
MESH = pl.DeviceIdType.MESH
DIRS = ((-1, 0), (1, 0), (0, -1), (0, 1), (-1, -1), (-1, 1), (1, -1), (1, 1))
CHUNK = 8


def hm(a, b):
    return 2.0 * a * b / jnp.maximum(a + b, 1e-30)


def over_planes(lo, hi, fn, chunk=CHUNK):
    for i in range(lo, hi, chunk):
        fn(i, min(chunk, hi - i))


def rolls(rows):
    def y_next(v):
        return pltpu.roll(v, rows - 1, 1)

    def y_prev(v):
        return pltpu.roll(v, 1, 1)

    def z_next(v):
        return pltpu.roll(v, 127, 2)

    def z_prev(v):
        return pltpu.roll(v, 1, 2)

    return y_next, y_prev, z_next, z_prev


def make_coefficients(k, cx, cy, cz, w, d, scale):
    planes, rows, _ = k.shape
    y_next, y_prev, z_next, z_prev = rolls(rows)
    cx[0] = scale * hm(k[0], k[1])

    def fn(i, n):
        here = k[pl.ds(i, n)]
        x = scale * hm(here, k[pl.ds(i + 1, n)])
        cx[pl.ds(i, n)] = x
        y = scale * hm(here, y_next(here))
        cy[pl.ds(i, n)] = y
        z = hm(here, z_next(here))
        lane = lax.broadcasted_iota(jnp.int32, z.shape, 2)
        z = jnp.where(lane < 127, z, 0.0)
        cz[pl.ds(i, n)] = z
        diag = STORE + x + cx[pl.ds(i - 1, n)] + y + y_prev(y) + z + z_prev(z)
        d[pl.ds(i, n)] = diag
        w[pl.ds(i, n)] = OMEGA / diag

    over_planes(1, planes - 1, fn)


def neighbour_sum(v, cx, cy, cz, i, n):
    y_next, y_prev, z_next, z_prev = rolls(v.shape[1])
    here = v[pl.ds(i, n)]
    y = cy[pl.ds(i, n)]
    z = cz[pl.ds(i, n)]
    total = cx[pl.ds(i, n)] * v[pl.ds(i + 1, n)] + cx[pl.ds(i - 1, n)] * v[pl.ds(i - 1, n)]
    total = total + (y * y_next(here) + y_prev(y * here))
    total = total + (z * z_next(here) + z_prev(z * here))
    return here, total


def sweep(src, dst, b, cx, cy, cz, w, lo, hi):
    def fn(i, n):
        here, total = neighbour_sum(src, cx, cy, cz, i, n)
        dst[pl.ds(i, n)] = (1.0 - OMEGA) * here + w[pl.ds(i, n)] * (b[pl.ds(i, n)] + total)

    over_planes(lo, hi, fn)


def restrict(src, off, tmp, dst, dst_off, cx_, cy_):
    for i in range(cx_):
        tmp[i] = 0.25 * (src[off + 2 * i, 0 : 2 * cy_] + src[off + 2 * i + 1, 0 : 2 * cy_])
        dst[dst_off + i, 0:cy_] = tmp[i, pl.ds(0, cy_, stride=2)] + tmp[i, pl.ds(1, cy_, stride=2)]


def edge_rows(extent, width, step):
    return range(extent - width, extent) if step > 0 else range(width)


def halo_rows(extent, rows, width, step):
    return range(rows - width, rows) if step > 0 else range(extent, extent + width)


def halo_planes(extent, off, width, step):
    return range(off - width, off) if step > 0 else range(off + extent, off + extent + width)


def flat(ref):
    planes, rows, lanes = ref.shape
    return ref.reshape(planes * rows, lanes)


def zero_halo(ref, extent_x, extent_y, off, width, low, high):
    planes, rows, lanes = ref.shape

    def zero(start, stop, first, last):
        if stop > start:
            ref[start:stop, first:last] = jnp.zeros((stop - start, last - first, lanes), jnp.float32)

    zero(0, planes, extent_y, rows)
    zero(0, off - width, 0, extent_y)
    zero(off + extent_x + width, planes, 0, extent_y)

    @pl.when(jnp.logical_not(low))
    def _():
        zero(off - width, off, 0, extent_y)

    @pl.when(jnp.logical_not(high))
    def _():
        zero(off + extent_x, off + extent_x + width, 0, extent_y)


def kernel(
    p_in, s_in, k_in, p_out, c1_out, b2, cx2, cy2, cz2, w2,
    k0, p0, s0, p1, p2, cx0, cy0, cz0, w0, d0,
    k1, b1, u1, v1, cx1, cy1, cz1, w1, d1,
    k2, d2,
    r0, r1, t0, t1,
    yk, ykr, yv, yvr, ym, ymr, ca, car, yc, ycr, cc, ccr, yd, ydr, cd, cdr,
    lsem, ssem, rsem,
):
    X, Y = p_in.shape[0], p_in.shape[1]
    nx, ny = lax.axis_size("gx"), lax.axis_size("gy")
    gx, gy = lax.axis_index("gx"), lax.axis_index("gy")
    H0, H1, H2 = 3, 3, 4
    X1, Y1, X2, Y2 = X // 2, Y // 2, X // 4, Y // 4

    def exists(d):
        dx, dy = d
        ok = None
        for coord, step, size in ((gx, dx, nx), (gy, dy, ny)):
            if step:
                one = (coord + step >= 0) & (coord + step < size)
                ok = one if ok is None else ok & one
        return ok

    here = {d: exists(d) for d in DIRS}

    def opposite(d):
        return (-d[0], -d[1])

    local = [
        pltpu.make_async_copy(src, dst.at[H0 : H0 + X, 0:Y], lsem.at[i])
        for i, (src, dst) in enumerate(((k_in, k0), (p_in, p0), (s_in, s0)))
    ]
    for copy in local:
        copy.start()

    barrier = pltpu.get_barrier_semaphore()
    for d in DIRS:

        @pl.when(here[d])
        def _():
            pl.semaphore_signal(
                barrier, inc=1, device_id={"gx": gx + d[0], "gy": gy + d[1]}, device_id_type=MESH
            )

    low, high = here[(-1, 0)], here[(1, 0)]
    zero_halo(k0, X, Y, H0, 3, low, high)
    zero_halo(p0, X, Y, H0, 3, low, high)
    zero_halo(s0, X, Y, H0, 2, low, high)
    zero_halo(k1, X1, Y1, H1, 3, low, high)
    zero_halo(b1, X1, Y1, H1, 2, low, high)
    zero_halo(k2, X2, Y2, H2, 4, low, high)
    zero_halo(b2, X2, Y2, H2, 3, low, high)

    counter = [0]

    def message(d, src, dst):
        slot = counter[0]
        counter[0] += 1
        copy = pltpu.make_async_remote_copy(
            src_ref=src, dst_ref=dst, send_sem=ssem.at[slot], recv_sem=rsem.at[slot],
            device_id={"gx": gx + d[0], "gy": gy + d[1]}, device_id_type=MESH,
        )

        @pl.when(here[d])
        def _():
            copy.start()

        return d, copy

    def receive(messages):
        for d, copy in messages:

            @pl.when(here[opposite(d)])
            def _():
                copy.wait_recv()

    def drain(messages):
        for d, copy in messages:

            @pl.when(here[d])
            def _():
                copy.wait_send()

    def part(ref, planes, rows):
        return ref.at[planes.start : planes.stop, 0:rows]

    R0, R1, R2 = k0.shape[1], k1.shape[1], k2.shape[1]

    def pack_side(stage, j, slot, ref, off, ex, ey, width, dy):
        for y in edge_rows(ey, width, dy):
            stage[j, slot : slot + ex] = flat(ref)[pl.ds(off * ref.shape[1] + y, ex, stride=ref.shape[1]), :]
            slot += ex
        return slot

    def unpack_side(stage, j, slot, ref, off, ex, ey, width, dy):
        for y in halo_rows(ey, ref.shape[1], width, dy):
            flat(ref)[pl.ds(off * ref.shape[1] + y, ex, stride=ref.shape[1]), :] = stage[j, slot : slot + ex]
            slot += ex
        return slot

    def pack_corner(stage, j, slot, ref, off, ex, ey, width, d):
        ys = edge_rows(ey, width, d[1])
        for x in edge_rows(ex, width, d[0]):
            stage[j, slot : slot + width] = ref[off + x, ys.start : ys.stop]
            slot += width
        return slot

    def unpack_corner(stage, j, slot, ref, off, ex, ey, width, d):
        ys = halo_rows(ey, ref.shape[1], width, d[1])
        for x in halo_planes(ex, off, width, d[0]):
            ref[x, ys.start : ys.stop] = stage[j, slot : slot + width]
            slot += width
        return slot

    def pack_sides(arrays, side):
        for j, dy in enumerate((-1, 1)):
            slot = 0
            for ref, off, ex, ey, width, _ in arrays:
                slot = pack_side(side, j, slot, ref, off, ex, ey, width, dy)

    def pack_corners(arrays, corner):
        for j, d in enumerate(DIRS[4:]):
            slot = 0
            for ref, off, ex, ey, _, width in arrays:
                slot = pack_corner(corner, j, slot, ref, off, ex, ey, width, d)

    def unpack_sides(arrays, side):
        for j, dy in enumerate((-1, 1)):

            @pl.when(here[(0, -dy)])
            def _():
                slot = 0
                for ref, off, ex, ey, width, _ in arrays:
                    slot = unpack_side(side, j, slot, ref, off, ex, ey, width, dy)

    def unpack_corners(arrays, corner):
        for j, d in enumerate(DIRS[4:]):

            @pl.when(here[opposite(d)])
            def _():
                slot = 0
                for ref, off, ex, ey, _, width in arrays:
                    slot = unpack_corner(corner, j, slot, ref, off, ex, ey, width, d)

    def send_sides(side, side_in):
        return [message((0, dy), side.at[j], side_in.at[j]) for j, dy in enumerate((-1, 1))]

    def send_corners(corner, corner_in):
        return [message(d, corner.at[j], corner_in.at[j]) for j, d in enumerate(DIRS[4:])]

    def send_planes(arrays):
        sent = []
        for ref, off, ex, ey, width, _ in arrays:
            for d in DIRS[:2]:
                planes = edge_rows(ex, width, d[0])
                src = ref.at[off + planes.start : off + planes.stop, 0:ey]
                sent.append(message(d, src, part(ref, halo_planes(ex, off, width, d[0]), ey)))
        return sent

    arrays_k = ((k0, H0, X, Y, 3, 2),)
    arrays_v = ((p0, H0, X, Y, 3, 2), (s0, H0, X, Y, 2, 1))
    arrays_m = ((k1, H1, X1, Y1, 3, 2), (k2, H2, X2, Y2, 4, 3))
    arrays_a = arrays_k + arrays_v + arrays_m
    arrays_c = ((b1, H1, X1, Y1, 2, 1),)
    arrays_d = ((b2, H2, X2, Y2, 3, 2),)
    for copy in local:
        copy.wait()
    restrict(k0, H0, t0, k1, H1, X1, Y1)
    restrict(k1, H1, t1, k2, H2, X2, Y2)
    pack_corners(arrays_a, ca)
    pack_sides(arrays_k, yk)
    pack_sides(arrays_v, yv)
    pack_sides(arrays_m, ym)
    one = lambda d: here[d].astype(jnp.int32)
    count = one(DIRS[0])
    for d in DIRS[1:]:
        count = count + one(d)
    pl.semaphore_wait(barrier, count)

    sent_k = send_corners(ca, car) + send_sides(yk, ykr) + send_planes(arrays_k)
    sent_v = send_sides(yv, yvr) + send_planes(arrays_v)
    sent_m = send_sides(ym, ymr) + send_planes(arrays_m)

    receive(sent_k)
    unpack_corners(arrays_a, car)
    unpack_sides(arrays_k, ykr)
    make_coefficients(k0, cx0, cy0, cz0, w0, d0, 1.0)
    receive(sent_v)
    unpack_sides(arrays_v, yvr)
    sweep(p0, p1, s0, cx0, cy0, cz0, w0, 1, X + 5)
    sweep(p1, p2, s0, cx0, cy0, cz0, w0, 2, X + 4)

    def residual0(i, n):
        value, total = neighbour_sum(p2, cx0, cy0, cz0, i, n)
        p_out[pl.ds(i - H0, n)] = value[:, 0:Y]
        r = s0[pl.ds(i, n)] + total - d0[pl.ds(i, n)] * value
        r0[pl.ds(i - H0, n)] = r[:, 0:Y]

    over_planes(H0, H0 + X, residual0)
    restrict(r0, 0, t0, b1, H1, X1, Y1)

    pack_corners(arrays_c, cc)
    pack_sides(arrays_c, yc)
    sent_c = send_corners(cc, ccr) + send_sides(yc, ycr) + send_planes(arrays_c)
    receive(sent_m)
    unpack_sides(arrays_m, ymr)
    make_coefficients(k1, cx1, cy1, cz1, w1, d1, 0.25)
    make_coefficients(k2, cx2, cy2, cz2, w2, d2, 0.0625)

    drain(sent_k + sent_v + sent_m)
    receive(sent_c)
    unpack_corners(arrays_c, ccr)
    unpack_sides(arrays_c, ycr)
    u1[1 : X1 + 5] = w1[1 : X1 + 5] * b1[1 : X1 + 5]
    sweep(u1, v1, b1, cx1, cy1, cz1, w1, 2, X1 + 4)

    def residual1(i, n):
        value, total = neighbour_sum(v1, cx1, cy1, cz1, i, n)
        c1_out[pl.ds(i - H1, n)] = value[:, 0:Y1]
        r = b1[pl.ds(i, n)] + total - d1[pl.ds(i, n)] * value
        r1[pl.ds(i - H1, n)] = r[:, 0:Y1]

    over_planes(H1, H1 + X1, residual1)
    restrict(r1, 0, t1, b2, H2, X2, Y2)

    pack_corners(arrays_d, cd)
    pack_sides(arrays_d, yd)
    sent_d = send_corners(cd, cdr) + send_sides(yd, ydr) + send_planes(arrays_d)
    drain(sent_c)
    receive(sent_d)
    unpack_corners(arrays_d, cdr)
    unpack_sides(arrays_d, ydr)

    drain(sent_d)


def finish(p_in, c1_in, b2, cx2, cy2, cz2, w2, p_out, c1_out, c2_out, u2, v2, c2, sem):
    off = (b2.shape[0] - c2.shape[0]) // 2
    X2, Y2 = c2.shape[0], c2.shape[1]
    first = pltpu.make_async_copy(p_in, p_out, sem.at[0])
    second = pltpu.make_async_copy(c1_in, c1_out, sem.at[1])
    first.start()
    second.start()
    u2[0] = jnp.zeros(u2.shape[1:], jnp.float32)
    u2[X2 + 7] = jnp.zeros(u2.shape[1:], jnp.float32)
    u2[1 : X2 + 7] = w2[1 : X2 + 7] * b2[1 : X2 + 7]
    sweep(u2, v2, b2, cx2, cy2, cz2, w2, 2, X2 + 6)
    sweep(v2, u2, b2, cx2, cy2, cz2, w2, 3, X2 + 5)
    value, total = neighbour_sum(u2, cx2, cy2, cz2, off, X2)
    value = (1.0 - OMEGA) * value + w2[off : off + X2] * (b2[off : off + X2] + total)
    c2[...] = value[:, 0:Y2]
    third = pltpu.make_async_copy(c2, c2_out, sem.at[2])
    third.start()
    first.wait()
    second.wait()
    third.wait()


MESSAGES = 20 + 8 + 8


def body(pressure_init, source, permeability):
    X, Y, Z = permeability.shape
    f32 = jnp.float32

    def vmem(*shape):
        return pltpu.VMEM(shape, f32)

    def level(x, y, off):
        return (x + 2 * off, y + 8, Z)

    l0, l1, l2 = level(X, Y, 3), level(X // 2, Y // 2, 3), level(X // 4, Y // 4, 4)
    scratch = (
        [vmem(*l0)] * 10
        + [vmem(*l1)] * 9
        + [vmem(*l2)] * 2
        + [vmem(X, Y, Z), vmem(X // 2, Y // 2, Z), vmem(X // 2, Y, Z), vmem(X // 4, Y // 2, Z)]
        + [vmem(2, 3 * X, Z)] * 2
        + [vmem(2, 5 * X, Z)] * 2
        + [vmem(2, 3 * (X // 2) + 4 * (X // 4), Z)] * 2
        + [vmem(4, 24, Z)] * 2
        + [vmem(2, 2 * (X // 2), Z)] * 2
        + [vmem(4, 8, Z)] * 2
        + [vmem(2, 16, Z)] * 2
        + [vmem(4, 8, Z)] * 2
        + [
            pltpu.SemaphoreType.DMA((3,)),
            pltpu.SemaphoreType.DMA((MESSAGES,)),
            pltpu.SemaphoreType.DMA((MESSAGES,)),
        ]
    )
    def out(*shape):
        return jax.ShapeDtypeStruct(shape, f32)

    whole = pl.BlockSpec(memory_space=pltpu.VMEM)
    far = pl.BlockSpec(memory_space=pltpu.HBM)
    fine, mid, coarse = out(X, Y, Z), out(X // 2, Y // 2, Z), out(X // 4, Y // 4, Z)
    parts = pl.pallas_call(
        kernel,
        out_shape=(fine, mid) + (out(*l2),) * 5,
        in_specs=[far] * 3,
        out_specs=[whole] * 7,
        scratch_shapes=scratch,
        compiler_params=pltpu.CompilerParams(
            collective_id=0, has_side_effects=True, vmem_limit_bytes=53 * 1024 * 1024
        ),
    )(pressure_init, source, permeability)
    return pl.pallas_call(
        finish,
        out_shape=(fine, mid, coarse),
        in_specs=[whole] * 7,
        out_specs=[far] * 3,
        scratch_shapes=[vmem(*l2), vmem(*l2), vmem(X // 4, Y // 4, Z), pltpu.SemaphoreType.DMA((3,))],
        compiler_params=pltpu.CompilerParams(vmem_limit_bytes=16 * 1024 * 1024),
    )(*parts)


def solution(mesh):
    spec = P("gx", "gy", None)
    return jax.shard_map(
        body, mesh=mesh, in_specs=(spec,) * 3, out_specs=(spec,) * 3, check_vma=False
    )
```
